32 devices in a mesh: groups: 2 (over x), fsdp: 8 (over z, y), head: 2 (over core).
Axes of the slice: x: 2, y: 2, z: 4, core: 2. Of those that a mesh axis runs over, the one named last changes fastest.
Arguments:
- activations: bfloat16 [4096, 16384], P(('groups', 'fsdp'), 'head'), parts along dimension 0, may hold values from -6 to 6
- queries: bfloat16 [4096, 8192], P(('groups', 'fsdp'), 'head'), parts along dimension 0, may hold values from -400 to 400
- w_key: bfloat16 [16384, 512], P('fsdp', 'head'), may hold values from -0.046875 to 0.046875
- w_value: bfloat16 [16384, 512], P('fsdp', 'head'), may hold values from -0.046875 to 0.046875
- request_pages: int32 [16], P('groups'), parts along dimension 0, may hold values from 1 to 7, 16 in all
- request_owner: int32 [16], P('groups'), parts along dimension 0, may hold values from 0 to 7, each once
Outputs:
- attended: bfloat16 [4096, 8192], P(('groups', 'fsdp'), 'head'), parts along dimension 0
- kv_cache: bfloat16 [112, 2, 128, 512], P(('groups', 'fsdp'), None, None, 'head'), parts along dimension 0
The draws below stay inside these ranges and needn't reach their ends.
There are 2 independent parts, one for each index of `groups`. The reference program is written for one: setup_inputs(seed, part) draws one part's arguments, and reference() takes and returns one part's arrays. A program takes and returns all parts, laid end to end along the dimension named above; an argument that names none is the same for every part. Nothing has to cross between parts.
Inputs may be any that keep to these rules, and one draw needn't show every extreme that they name: `request_pages`: the requests' page counts sum to 16, and the longest has exactly 7 pages. `request_owner`: each decode device owns exactly one request.
All inputs are finite; a program needn't handle non-finite values.
Results may differ from the reference program's by a relative error of at most 0.012.
The reference program's roundings to bfloat16 on the way count: a program that leaves them out, or rounds other values in their place, can miss the bound.
Values may be sent and summed in bfloat16 or wider, within the bound.
A program may use at most 128 MiB of HBM per device.

```python
import math
import jax
import jax.numpy as jnp
import numpy as np
from jax import lax

D = 16384
QH = 64
KVH = 4
HD = 128
PAGE = 128
SPAN = 3
TOK_DEV = 256
PAGES_DEV = 2
CAP = 7
REQUESTS = 8
TOKENS = 2048
N_FSDP = 8


def draw_queries(key, part):
    key = jax.random.fold_in(key, 11)
    base_key, scale_key = jax.random.split(key)
    base = jnp.clip(jax.random.normal(base_key, (TOKENS, QH, HD), jnp.float32), -6.0, 6.0)
    row_scale = jnp.exp(jax.random.uniform(scale_key, (TOKENS, QH, 1), jnp.float32, math.log(0.5), math.log(2.0)))
    return (base * row_scale).reshape(TOKENS, QH * HD).astype(jnp.bfloat16)


def shard_levels(key, dims, cuts, smallest, largest):
    loudness = 1.0
    for axis_at, parts in cuts:
        heights = jax.random.uniform(jax.random.fold_in(jax.random.fold_in(key, 6), axis_at), (parts,), jnp.float32, smallest / len(cuts), largest / len(cuts))
        loudness = loudness * jnp.repeat(jnp.exp(heights), dims[axis_at] // parts).reshape((-1,) + (1,) * (len(dims) - 1 - axis_at))
    return loudness


def profile(count, total, most, lean):
    loads = [(1 << 20) // math.isqrt(rank ** lean) + 1 for rank in range(2, count + 1)]
    surplus, counts = total - most - (count - 1), [1] * (count - 1)
    while surplus > 0:
        free = [i for i in range(count - 1) if counts[i] < most]
        pool, left = sum([loads[i] for i in free]), surplus
        for i in free:
            addition = min(most - counts[i], max(1, left * loads[i] // pool), surplus)
            counts[i] = counts[i] + addition
            surplus = surplus - addition
    return np.array([most] + counts)


def uneven_parts(rng, amount, total, limit, skew):
    if amount == 2:
        one = jax.random.randint(rng, (), max(1, total - limit), min(limit, total - 1) + 1)
        return jnp.stack([one, total - one])
    sizes = jnp.asarray(profile(amount, total, limit, skew), jnp.int32)
    pairs = (amount - 1) // 2
    source_of, receiver = sizes[1:1 + 2 * pairs:2], sizes[2:2 + 2 * pairs:2]
    room = jnp.minimum(source_of - 1, limit - receiver)
    shifted = jax.random.randint(jax.random.fold_in(rng, 1), (pairs,), 0, 1 << 20) % (room + 1)
    sizes = sizes.at[1:1 + 2 * pairs:2].set(source_of - shifted).at[2:2 + 2 * pairs:2].set(receiver + shifted)
    return sizes[jax.random.permutation(jax.random.fold_in(rng, 2), amount)]


def gaussian(key, extent, spread, bound, shards=(), held_as=jnp.bfloat16):
    drawn = jax.random.normal(key, extent, jnp.float32) * spread
    if len(shards) > 0:
        drawn = shard_levels(key, extent, shards, -0.22, 0.18) * drawn
    return jnp.clip(drawn, min=-bound, max=bound).astype(held_as)


def setup_inputs(seed: int = 0, part: int = 0) -> dict:
    key_list = jax.random.split(jax.random.key(seed), 7)
    part_splits = jax.random.split(jax.random.fold_in(key_list[6], part), 7)
    activations = gaussian(part_splits[0], (TOKENS, D), 1.0, 6.0, ((0, 8), (1, 2)))
    queries = draw_queries(jax.random.fold_in(jax.random.fold_in(key_list[6], part), 71), part)
    w_key = gaussian(key_list[2], (D, KVH * HD), D ** -0.5, 0.046875, ((0, 8), (1, 2)))
    w_value = gaussian(key_list[3], (D, KVH * HD), D ** -0.5, 0.046875, ((0, 8), (1, 2)))
    request_pages = uneven_parts(part_splits[4], REQUESTS, N_FSDP * PAGES_DEV, CAP, 2).astype(jnp.int32)
    request_owner = jax.random.permutation(part_splits[5], N_FSDP).astype(jnp.int32)
    return {"activations": activations, "queries": queries, "w_key": w_key, "w_value": w_value, "request_pages": request_pages, "request_owner": request_owner}


def page_documents(request_pages, page_count):
    doc_ends = jnp.cumsum(request_pages).astype(jnp.int32)
    page_index = jnp.arange(page_count, dtype=jnp.int32)
    return jnp.sum((doc_ends[None, :] <= page_index[:, None]).astype(jnp.int32), axis=1).astype(jnp.int32)


def reference(activations, queries, w_key, w_value, request_pages, request_owner):
    key_rows = jnp.dot(activations, w_key, preferred_element_type=jnp.float32).astype(jnp.bfloat16)
    value_rows = jnp.dot(activations, w_value, preferred_element_type=jnp.float32).astype(jnp.bfloat16)
    page_count = TOKENS // PAGE
    page_doc = page_documents(request_pages, page_count)
    token_doc = jnp.repeat(page_doc, PAGE).astype(jnp.int32)
    per_group = QH // KVH
    margin = SPAN * TOK_DEV
    window = margin + TOK_DEV
    padded_keys = jnp.concatenate([jnp.zeros((margin, KVH * HD), jnp.bfloat16), key_rows], axis=0)
    padded_values = jnp.concatenate([jnp.zeros((margin, KVH * HD), jnp.bfloat16), value_rows], axis=0)
    padded_docs = jnp.concatenate([jnp.full((margin,), -1, jnp.int32), token_doc], axis=0)
    score_scale = HD ** -0.5

    def attend(block_index):
        offset = (block_index * TOK_DEV).astype(jnp.int32)
        zero_index = jnp.zeros((), jnp.int32)
        query_block = lax.dynamic_slice(queries, (offset, zero_index), (TOK_DEV, QH * HD))
        query_block = query_block.astype(jnp.float32).reshape(TOK_DEV, KVH, per_group, HD)
        key_block = lax.dynamic_slice(padded_keys, (offset, zero_index), (window, KVH * HD))
        key_block = key_block.astype(jnp.float32).reshape(window, KVH, HD)
        value_block = lax.dynamic_slice(padded_values, (offset, zero_index), (window, KVH * HD))
        value_block = value_block.astype(jnp.float32).reshape(window, KVH, HD)
        query_docs = lax.dynamic_slice(padded_docs, (offset + margin,), (TOK_DEV,))
        key_docs = lax.dynamic_slice(padded_docs, (offset,), (window,))
        query_pos = offset + margin + jnp.arange(TOK_DEV, dtype=jnp.int32)
        key_pos = offset + jnp.arange(window, dtype=jnp.int32)
        visible = (key_docs[None, :] == query_docs[:, None]) & (key_pos[None, :] <= query_pos[:, None])
        scores = jnp.einsum("tgqd,sgd->gqts", query_block, key_block) * score_scale
        scores = jnp.where(visible[None, None], scores, -1e30)
        row_top = jnp.max(scores, axis=-1, keepdims=True)
        expo = jnp.where(visible[None, None], jnp.exp(scores - row_top), 0.0)
        row_total = jnp.sum(expo, axis=-1)
        rounded = lax.optimization_barrier(expo.astype(jnp.bfloat16))
        weighted = jnp.einsum("gqts,sgd->tgqd", rounded.astype(jnp.float32), value_block)
        result = weighted / jnp.transpose(row_total, (2, 0, 1))[..., None]
        return result.reshape(TOK_DEV, QH * HD).astype(jnp.bfloat16)

    attended = lax.map(attend, jnp.arange(N_FSDP, dtype=jnp.int32)).reshape(TOKENS, QH * HD)
    doc_ends = jnp.cumsum(request_pages).astype(jnp.int32)
    doc_begins = doc_ends - request_pages
    page_index = jnp.arange(page_count, dtype=jnp.int32)
    slots = (request_owner[page_doc] * CAP + page_index - doc_begins[page_doc]).astype(jnp.int32)
    page_data = jnp.stack([key_rows.reshape(page_count, PAGE, KVH * HD), value_rows.reshape(page_count, PAGE, KVH * HD)], axis=1)
    kv_cache = jnp.zeros((N_FSDP * CAP, 2, PAGE, KVH * HD), jnp.bfloat16).at[slots].set(page_data)
    return attended, kv_cache
```

```python
import jax
import jax.numpy as jnp
from jax import lax
from jax.sharding import PartitionSpec as P

QH = 64
KVH = 4
HD = 128
PAGE = 128
SPAN = 3
FSDP = ("z", "y")
PLANE = ("groups", "y")


def shifted(array, axis, by):
    count = lax.axis_size("z") * lax.axis_size("y")
    pairs = [(i, i + by) for i in range(count) if 0 <= i + by < count]
    return lax.ppermute(array, axis, pairs)


def token_docs(first_tok, count, doc_ends):
    positions = first_tok + jnp.arange(count, dtype=jnp.int32)
    pages = positions // PAGE
    found = jnp.sum((doc_ends[None, :] <= pages[:, None]).astype(jnp.int32), axis=1)
    return (jnp.where(positions >= 0, found, -1), positions)


def page_slot(global_pages, doc_ends, doc_begins, request_owner, cache_pages):
    count = doc_ends.shape[0]
    found = jnp.sum((doc_ends[None, :] <= global_pages[:, None]).astype(jnp.int32), axis=1)
    matched = found[:, None] == jnp.arange(count, dtype=jnp.int32)[None, :]
    owner_dev = jnp.sum(jnp.where(matched, request_owner[None, :], 0), axis=1)
    doc_begin = jnp.sum(jnp.where(matched, doc_begins[None, :], 0), axis=1)
    return owner_dev * cache_pages + global_pages - doc_begin


def project(activations, w_key, w_value):
    tok_rows, half = activations.shape
    n_groups, n_y = lax.axis_size("groups"), lax.axis_size("y")
    depth, width = w_key.shape
    part = depth // n_groups
    n_z = half // (part * n_y * n_groups)
    split = activations.reshape(tok_rows, n_z, n_y, n_groups, part)
    split = jnp.transpose(split, (3, 2, 0, 1, 4)).reshape(n_groups * n_y, tok_rows, n_z * part)
    mine = lax.all_to_all(split, PLANE, split_axis=0, concat_axis=0, tiled=True)
    mine = mine.reshape(n_groups * n_y * tok_rows, n_z * part)
    both = lax.all_gather(mine, "head", axis=1, tiled=True)
    group = lax.axis_index("groups")
    weights = jnp.concatenate([w_key, w_value], axis=1)
    weights = lax.dynamic_slice(weights, (group * part, 0), (part, 2 * width))
    weights = lax.all_gather(weights, "z", axis=0, tiled=True)
    partial = jnp.dot(both, weights, preferred_element_type=jnp.float32)
    rows = lax.psum_scatter(partial, PLANE, scatter_dimension=0, tiled=True)
    rows = rows.astype(jnp.bfloat16)
    return rows[:, :width], rows[:, width:]


def masked_scores(query_head, key_head, visible, score_scale):
    scores = (
        jnp.einsum("tqd,sd->qts", query_head, key_head, preferred_element_type=jnp.float32)
        * score_scale
    )
    return jnp.where(visible[None], scores, -1e30)


def per_device(activations, queries, w_key, w_value, request_pages, request_owner):
    tok_rows = activations.shape[0]
    width_kv = w_key.shape[1]
    kv_here = width_kv // HD
    per_group = QH // KVH
    n_dev = lax.axis_size("z") * lax.axis_size("y")
    my_index = lax.axis_index(FSDP)
    score_scale = HD ** (-0.5)
    key_rows, value_rows = project(activations, w_key, w_value)
    doc_ends = jnp.cumsum(request_pages)
    doc_begins = doc_ends - request_pages
    first_tok = my_index * tok_rows
    query_docs, query_pos = token_docs(first_tok, tok_rows, doc_ends)
    blocks = [(key_rows, value_rows, first_tok)]
    for distance in range(1, SPAN + 1):
        near_k, near_v = shifted((key_rows, value_rows), FSDP, distance)
        blocks.append((near_k, near_v, first_tok - distance * tok_rows))
    described = []
    for index, (block_k, block_v, block_first) in enumerate(blocks):
        key_docs, key_pos = token_docs(block_first, tok_rows, doc_ends)
        visible = (key_docs[None, :] == query_docs[:, None]) & (
            key_pos[None, :] <= query_pos[:, None]
        )
        live = None if index == 0 else key_docs[tok_rows - 1] == query_docs[0]
        described.append((block_k, block_v, visible, live))
    query_all = queries.reshape(tok_rows, kv_here, per_group, HD)
    head_outputs = []
    for kv_index in range(kv_here):
        query_head = query_all[:, kv_index]
        low = kv_index * HD
        key_head = jnp.concatenate([item[0][:, low : low + HD] for item in described], 0)
        value_head = jnp.concatenate([item[1][:, low : low + HD] for item in described], 0)
        visible = jnp.concatenate([item[2] for item in described], 1)
        scores = masked_scores(query_head, key_head, visible, score_scale)
        row_top = jnp.max(scores, axis=-1, keepdims=True)
        expo = jnp.where(visible[None], jnp.exp(scores - row_top), 0.0)
        row_total = jnp.sum(expo, axis=-1)
        weights = expo.astype(jnp.bfloat16)
        weighted = jnp.einsum(
            "qts,sd->tqd", weights, value_head, preferred_element_type=jnp.float32
        )
        head_outputs.append(weighted / jnp.transpose(row_total, (1, 0))[:, :, None])
    attended = (
        jnp.stack(head_outputs, axis=1)
        .reshape(tok_rows, kv_here * per_group * HD)
        .astype(jnp.bfloat16)
    )
    pages_here = tok_rows // PAGE
    cache_pages = SPAN * pages_here + 1
    page_data = jnp.stack(
        [
            key_rows.reshape(pages_here, PAGE, width_kv),
            value_rows.reshape(pages_here, PAGE, width_kv),
        ],
        axis=1,
    )
    flat_pages = page_data.reshape(pages_here, 2 * PAGE * width_kv)
    slot_ids = jnp.arange(cache_pages, dtype=jnp.int32)
    own_pages = my_index * pages_here + jnp.arange(pages_here, dtype=jnp.int32)
    target = page_slot(own_pages, doc_ends, doc_begins, request_owner, cache_pages) // cache_pages
    routed = target[None, :] == jnp.arange(n_dev, dtype=jnp.int32)[:, None]
    outgoing = jnp.where(routed[:, :, None], flat_pages[None], jnp.zeros((), jnp.bfloat16))
    incoming = lax.all_to_all(outgoing, FSDP, split_axis=0, concat_axis=0, tiled=True)
    incoming = incoming.reshape(n_dev * pages_here, 2 * PAGE * width_kv)
    source_pages = jnp.arange(n_dev * pages_here, dtype=jnp.int32)
    local_slot = (
        page_slot(source_pages, doc_ends, doc_begins, request_owner, cache_pages)
        - my_index * cache_pages
    )
    selector = (local_slot[None, :] == slot_ids[:, None]).astype(jnp.bfloat16)
    cache_sum = jnp.dot(selector, incoming, preferred_element_type=jnp.float32)
    kv_cache = cache_sum.astype(jnp.bfloat16).reshape(cache_pages, 2, PAGE, width_kv)
    return (attended, kv_cache)


def solution(mesh):
    groups, fsdp, head = mesh.devices.shape
    n_y = max(1, 4 // groups)
    fine = jax.sharding.Mesh(
        mesh.devices.reshape(groups, fsdp // n_y, n_y, head), ("groups", "z", "y", "head")
    )
    tokens = ("groups", "z", "y")
    return jax.shard_map(
        per_device,
        mesh=fine,
        in_specs=(
            P(tokens, "head"),
            P(tokens, "head"),
            P(FSDP, "head"),
            P(FSDP, "head"),
            P("groups"),
            P("groups"),
        ),
        out_specs=(P(tokens, "head"), P(tokens, None, None, "head")),
        check_vma=False,
    )
```

```python
import functools
import jax
import jax.numpy as jnp
from jax import lax
from jax.experimental import pallas as pl
from jax.experimental.pallas import tpu as pltpu
from jax.sharding import PartitionSpec as P

QH = 64
KVH = 4
HD = 128
PAGE = 128
SPAN = 3
PLANE = 4


def rows_kernel(
    n_groups, n_z, n_y, acts, w_key, w_value, out, abuf, wbuf, acc, sbuf, rbuf, gbuf,
    w_right, w_left, w_recv, a_send, a_recv, f_send, f_recv, r_send, r_recv,
    g_right, g_left, g_cross, g_recv, c_recv, loc_w, loc_a, loc_out,
):
    group = lax.axis_index("groups")
    fsdp = lax.axis_index("fsdp")
    head = lax.axis_index("head")
    z = fsdp // n_y
    y = fsdp % n_y
    me = group * n_y + y
    rows = acts.shape[0]
    part = w_key.shape[0] // n_groups
    width = w_key.shape[1]
    half_z = n_z // 2
    sibling = (group, fsdp, 1 - head)
    right = (group, fsdp + n_y, head)
    left = (group, fsdp - n_y, head)
    has_right = z < n_z - 1
    has_left = z > 0

    def chip(p):
        return (p // n_y, z * n_y + p % n_y, head)

    def remote(src, dst, send, recv, dev):
        return pltpu.make_async_remote_copy(
            src_ref=src, dst_ref=dst, send_sem=send, recv_sem=recv,
            device_id=dev, device_id_type=pl.DeviceIdType.MESH,
        )

    barrier = pltpu.get_barrier_semaphore()

    def greet(dev):
        pl.semaphore_signal(barrier, inc=1, device_id=dev, device_id_type=pl.DeviceIdType.MESH)

    for j in range(1, PLANE):
        greet(chip((me + j) % PLANE))
    greet(sibling)
    pl.when(has_right)(lambda: greet(right))
    pl.when(has_left)(lambda: greet(left))
    pl.semaphore_wait(barrier, PLANE + jnp.minimum(z, 1) + jnp.minimum(n_z - 1 - z, 1))

    mine = pl.ds(pl.multiple_of(group * part, part), part)
    w_own = [w_key.at[mine, :], w_value.at[mine, :]]

    def w_copy(block, c, dev, send, own):
        src = w_own[c] if own else wbuf.at[block, c]
        return remote(src, wbuf.at[block, c], send.at[block, c], w_recv.at[block, c], dev)

    for c in range(2):
        pl.when(has_right)(lambda c=c: w_copy(z, c, right, w_right, True).start())
        pl.when(has_left)(lambda c=c: w_copy(z, c, left, w_left, True).start())

    def cols(zz, p):
        start = ((zz * n_y + p % n_y) * n_groups + p // n_y) * part
        return acts.at[:, pl.ds(pl.multiple_of(start, part), part)]

    def a_copy(zz, j):
        p = (me + j) % PLANE
        return remote(
            cols(zz, p), abuf.at[head * half_z + zz, me], a_send.at[j, zz], a_recv.at[j, zz], chip(p)
        )

    def a_arrived(zz, j):
        q = (me + PLANE - j) % PLANE
        return remote(
            cols(zz, me), abuf.at[head * half_z + zz, q], a_send.at[j, zz], a_recv.at[j, zz], chip(q)
        )

    def f_copy(zz, j):
        q = (me + PLANE - j) % PLANE
        slot = abuf.at[head * half_z + zz, q]
        src = cols(zz, me) if j == 0 else slot
        return remote(src, slot, f_send.at[j, zz], f_recv.at[j, zz], sibling)

    def f_arrived(zz, j):
        q = (me + PLANE - j) % PLANE
        slot = abuf.at[(1 - head) * half_z + zz, q]
        return remote(slot, slot, f_send.at[j, zz], f_recv.at[j, zz], sibling)

    def own_a(zz):
        return pltpu.make_async_copy(cols(zz, me), abuf.at[head * half_z + zz, me], loc_a.at[zz])

    def own_w(c):
        return pltpu.make_async_copy(w_own[c], wbuf.at[z, c], loc_w.at[c])

    @pl.loop(0, half_z)
    def _(zz):
        for j in range(1, PLANE):
            a_copy(zz, j).start()

    @pl.loop(0, half_z)
    def _(zz):
        own_a(zz).start()
        f_copy(zz, 0).start()

    for c in range(2):
        own_w(c).start()
    acc[...] = jnp.zeros_like(acc)

    def w_step(s, forward):
        for c in range(2):
            from_left = z - 1 - s
            from_right = z + 1 + s

            @pl.when(from_left >= 0)
            def _():
                w_copy(from_left, c, right, w_right, False).wait_recv()
                if forward:
                    pl.when(has_right)(lambda: w_copy(from_left, c, right, w_right, False).start())

            @pl.when(from_right <= n_z - 1)
            def _():
                w_copy(from_right, c, left, w_left, False).wait_recv()
                if forward:
                    pl.when(has_left)(lambda: w_copy(from_right, c, left, w_left, False).start())

    @pl.loop(0, n_z - 2)
    def _(s):
        w_step(s, True)

    @pl.loop(0, half_z)
    def _(zz):
        for j in range(1, PLANE):
            a_arrived(zz, j).wait_recv()
            f_copy(zz, j).start()

    for c in range(2):
        own_w(c).wait()

    @pl.loop(0, half_z)
    def _(zz):
        own_a(zz).wait()

    @pl.loop(0, half_z)
    def _(zz):
        for j in range(PLANE):
            f_arrived(zz, j).wait_recv()

    def multiply(block):
        @pl.loop(0, PLANE)
        def _(p):
            for c in range(2):
                acc[p, :, c * width : (c + 1) * width] += jnp.dot(
                    abuf[block, p], wbuf[block, c], preferred_element_type=jnp.float32
                )

    @pl.loop(0, n_z)
    def _(block):
        pl.when((block - z < n_z - 1) & (z - block < n_z - 1))(lambda: multiply(block))

    w_step(n_z - 2, False)
    pl.when(z == 0)(lambda: multiply(n_z - 1))
    pl.when(z == n_z - 1)(lambda: multiply(0))

    def r_copy(j):
        p = (me + j) % PLANE
        return remote(sbuf.at[j - 1], rbuf.at[j - 1], r_send.at[j], r_recv.at[j], chip(p))

    for j in (2, 1, 3):
        sbuf[j - 1] = acc[(me + j) % PLANE].astype(jnp.bfloat16)
        r_copy(j).start()
    total = acc[me]
    for j in (1, 3, 2):
        r_copy(j).wait_recv()
        total += rbuf[j - 1].astype(jnp.float32)
    gbuf[fsdp] = total.astype(jnp.bfloat16)

    def g_copy(zz, dev, send, recv):
        slot = gbuf.at[zz * n_y + y]
        return remote(slot, slot, send.at[zz], recv.at[zz], dev)

    cross = (group, z * n_y + (n_y - 1 - y), head)

    def g_start(zz, to_right, to_left):
        if to_right:
            pl.when(has_right)(lambda: g_copy(zz, right, g_right, g_recv).start())
        if to_left:
            pl.when(has_left)(lambda: g_copy(zz, left, g_left, g_recv).start())
        if n_y == 2:
            g_copy(zz, cross, g_cross, c_recv).start()

    g_start(z, True, True)

    @pl.loop(0, n_z - 1)
    def _(s):
        from_left = z - 1 - s
        from_right = z + 1 + s

        @pl.when(from_left >= 0)
        def _():
            g_copy(from_left, right, g_right, g_recv).wait_recv()
            g_start(from_left, True, False)

        @pl.when(from_right <= n_z - 1)
        def _():
            g_copy(from_right, left, g_left, g_recv).wait_recv()
            g_start(from_right, False, True)

    if n_y == 2:
        @pl.loop(0, n_z)
        def _(zz):
            slot = gbuf.at[zz * n_y + (1 - y)]
            remote(slot, slot, g_cross.at[zz], c_recv.at[zz], cross).wait_recv()

    done = pltpu.make_async_copy(gbuf, out, loc_out)
    done.start()

    for j in range(1, PLANE):
        r_copy(j).wait_send()

    @pl.loop(0, half_z)
    def _(zz):
        for j in range(1, PLANE):
            a_copy(zz, j).wait_send()
        for j in range(PLANE):
            f_copy(zz, j).wait_send()

    @pl.loop(0, n_z)
    def _(block):
        @pl.when((block <= z) & has_right)
        def _():
            for c in range(2):
                w_copy(block, c, right, w_right, False).wait_send()
            g_copy(block, right, g_right, g_recv).wait_send()

        @pl.when((block >= z) & has_left)
        def _():
            for c in range(2):
                w_copy(block, c, left, w_left, False).wait_send()
            g_copy(block, left, g_left, g_recv).wait_send()

        if n_y == 2:
            g_copy(block, cross, g_cross, c_recv).wait_send()

    done.wait()


def project(mesh_sizes, activations, w_key, w_value):
    n_groups, n_fsdp = mesh_sizes
    n_y = PLANE // n_groups
    n_z = n_fsdp // n_y
    rows = activations.shape[0]
    depth, width = w_key.shape
    part = depth // n_groups
    any_space = pl.BlockSpec(memory_space=pl.ANY)
    dma = pltpu.SemaphoreType.DMA
    half_z = n_z // 2
    return pl.pallas_call(
        functools.partial(rows_kernel, n_groups, n_z, n_y),
        out_shape=jax.ShapeDtypeStruct((n_fsdp, rows, 2 * width), jnp.bfloat16),
        in_specs=[any_space] * 3,
        out_specs=any_space,
        scratch_shapes=[
            pltpu.VMEM((n_z, PLANE, rows, part), jnp.bfloat16),
            pltpu.VMEM((n_z, 2, part, width), jnp.bfloat16),
            pltpu.VMEM((PLANE, rows, 2 * width), jnp.float32),
            pltpu.VMEM((PLANE - 1, rows, 2 * width), jnp.bfloat16),
            pltpu.VMEM((PLANE - 1, rows, 2 * width), jnp.bfloat16),
            pltpu.VMEM((n_fsdp, rows, 2 * width), jnp.bfloat16),
            dma((n_z, 2)),
            dma((n_z, 2)),
            dma((n_z, 2)),
            dma((PLANE, half_z)),
            dma((PLANE, half_z)),
            dma((PLANE, half_z)),
            dma((PLANE, half_z)),
            dma((PLANE,)),
            dma((PLANE,)),
            dma((n_z,)),
            dma((n_z,)),
            dma((n_z,)),
            dma((n_z,)),
            dma((n_z,)),
            dma((2,)),
            dma((half_z,)),
            dma,
        ],
        compiler_params=pltpu.CompilerParams(
            collective_id=0, has_side_effects=True, vmem_limit_bytes=48 * 2**20
        ),
    )(activations, w_key, w_value)


def token_docs(first_tok, count, doc_ends):
    positions = first_tok + jnp.arange(count, dtype=jnp.int32)
    pages = positions // PAGE
    found = jnp.sum((doc_ends[None, :] <= pages[:, None]).astype(jnp.int32), axis=1)
    return (jnp.where(positions >= 0, found, -1), positions)


def masked_scores(query_head, key_head, visible, score_scale):
    scores = (
        jnp.einsum("tqd,sd->qts", query_head, key_head, preferred_element_type=jnp.float32)
        * score_scale
    )
    return jnp.where(visible[None], scores, -1e30)


def per_device(mesh_sizes, activations, queries, w_key, w_value, request_pages, request_owner):
    tok_rows = activations.shape[0]
    width_kv = w_key.shape[1]
    kv_here = width_kv // HD
    per_group = QH // KVH
    my_index = lax.axis_index("fsdp")
    score_scale = HD ** (-0.5)
    gathered = project(mesh_sizes, activations, w_key, w_value)
    gathered = gathered.reshape(-1, 2 * width_kv)
    doc_ends = jnp.cumsum(request_pages)
    doc_begins = doc_ends - request_pages
    first_tok = my_index * tok_rows
    query_docs, query_pos = token_docs(first_tok, tok_rows, doc_ends)
    margin = SPAN * tok_rows
    padded = jnp.concatenate([jnp.zeros((margin, 2 * width_kv), jnp.bfloat16), gathered], axis=0)
    window = lax.dynamic_slice(padded, (first_tok, 0), (margin + tok_rows, 2 * width_kv))
    key_docs, key_pos = token_docs(first_tok - margin, margin + tok_rows, doc_ends)
    visible = (key_docs[None, :] == query_docs[:, None]) & (key_pos[None, :] <= query_pos[:, None])
    query_all = queries.reshape(tok_rows, kv_here, per_group, HD)
    head_outputs = []
    for kv_index in range(kv_here):
        query_head = query_all[:, kv_index]
        low = kv_index * HD
        key_head = window[:, low : low + HD]
        value_head = window[:, width_kv + low : width_kv + low + HD]
        scores = masked_scores(query_head, key_head, visible, score_scale)
        row_top = jnp.max(scores, axis=-1, keepdims=True)
        expo = jnp.where(visible[None], jnp.exp(scores - row_top), 0.0)
        row_total = jnp.sum(expo, axis=-1)
        weights = expo.astype(jnp.bfloat16)
        weighted = jnp.einsum(
            "qts,sd->tqd", weights, value_head, preferred_element_type=jnp.float32
        )
        head_outputs.append(weighted / jnp.transpose(row_total, (1, 0))[:, :, None])
    attended = (
        jnp.stack(head_outputs, axis=1)
        .reshape(tok_rows, kv_here * per_group * HD)
        .astype(jnp.bfloat16)
    )
    pages_here = tok_rows // PAGE
    cache_pages = SPAN * pages_here + 1
    owned = request_owner == my_index
    begin = jnp.sum(jnp.where(owned, doc_begins, 0))
    count = jnp.sum(jnp.where(owned, request_pages, 0))
    tail = jnp.zeros((cache_pages * PAGE, 2 * width_kv), jnp.bfloat16)
    pages = lax.dynamic_slice(
        jnp.concatenate([gathered, tail], axis=0),
        (begin * PAGE, 0),
        (cache_pages * PAGE, 2 * width_kv),
    ).reshape(cache_pages, PAGE, 2, width_kv)
    held = jnp.arange(cache_pages, dtype=jnp.int32) < count
    kv_cache = jnp.where(held[:, None, None, None], jnp.transpose(pages, (0, 2, 1, 3)), 0)
    kv_cache = kv_cache.astype(jnp.bfloat16)
    return (attended, kv_cache)


def solution(mesh):
    mesh_sizes = (mesh.shape["groups"], mesh.shape["fsdp"])
    return jax.shard_map(
        functools.partial(per_device, mesh_sizes),
        mesh=mesh,
        in_specs=(
            P(("groups", "fsdp"), "head"),
            P(("groups", "fsdp"), "head"),
            P("fsdp", "head"),
            P("fsdp", "head"),
            P("groups"),
            P("groups"),
        ),
        out_specs=(P(("groups", "fsdp"), "head"), P(("groups", "fsdp"), None, None, "head")),
        check_vma=False,
    )
```

```python
import functools
import jax
import jax.numpy as jnp
from jax import lax
from jax.experimental import pallas as pl
from jax.experimental.pallas import tpu as pltpu
from jax.sharding import PartitionSpec as P

HD = 128
PAGE = 128
SPAN = 3
PLANE = 4


def rows_kernel(
    n_groups, n_z, n_y, acts, w_key, w_value, out, abuf, wbuf, acc, sbuf, rbuf, gbuf,
    w_right, w_left, w_recv, a_send, a_recv, f_send, f_recv, r_send, r_recv,
    g_right, g_left, g_cross, g_recv, c_recv, loc_w, loc_a, loc_out,
):
    group = lax.axis_index("groups")
    fsdp = lax.axis_index("fsdp")
    head = lax.axis_index("head")
    z = fsdp // n_y
    y = fsdp % n_y
    me = group * n_y + y
    rows = acts.shape[0]
    part = w_key.shape[0] // n_groups
    width = w_key.shape[1]
    half_z = n_z // 2
    sibling = (group, fsdp, 1 - head)
    right = (group, fsdp + n_y, head)
    left = (group, fsdp - n_y, head)
    has_right = z < n_z - 1
    has_left = z > 0

    def chip(p):
        return (p // n_y, z * n_y + p % n_y, head)

    def remote(src, dst, send, recv, dev):
        return pltpu.make_async_remote_copy(
            src_ref=src, dst_ref=dst, send_sem=send, recv_sem=recv,
            device_id=dev, device_id_type=pl.DeviceIdType.MESH,
        )

    barrier = pltpu.get_barrier_semaphore()

    def greet(dev):
        pl.semaphore_signal(barrier, inc=1, device_id=dev, device_id_type=pl.DeviceIdType.MESH)

    for j in range(1, PLANE):
        greet(chip((me + j) % PLANE))
    greet(sibling)
    pl.when(has_right)(lambda: greet(right))
    pl.when(has_left)(lambda: greet(left))
    pl.semaphore_wait(barrier, PLANE + jnp.minimum(z, 1) + jnp.minimum(n_z - 1 - z, 1))

    mine = pl.ds(pl.multiple_of(group * part, part), part)
    w_own = [w_key.at[mine, :], w_value.at[mine, :]]

    def w_copy(block, c, dev, send, own):
        src = w_own[c] if own else wbuf.at[block, c]
        return remote(src, wbuf.at[block, c], send.at[block, c], w_recv.at[block, c], dev)

    for c in range(2):
        pl.when(has_right)(lambda c=c: w_copy(z, c, right, w_right, True).start())
        pl.when(has_left)(lambda c=c: w_copy(z, c, left, w_left, True).start())

    def cols(zz, p):
        start = ((zz * n_y + p % n_y) * n_groups + p // n_y) * part
        return acts.at[:, pl.ds(pl.multiple_of(start, part), part)]

    def a_copy(zz, j):
        p = (me + j) % PLANE
        return remote(
            cols(zz, p), abuf.at[head * half_z + zz, me], a_send.at[j, zz], a_recv.at[j, zz], chip(p)
        )

    def a_arrived(zz, j):
        q = (me + PLANE - j) % PLANE
        return remote(
            cols(zz, me), abuf.at[head * half_z + zz, q], a_send.at[j, zz], a_recv.at[j, zz], chip(q)
        )

    def f_copy(zz, j):
        q = (me + PLANE - j) % PLANE
        slot = abuf.at[head * half_z + zz, q]
        src = cols(zz, me) if j == 0 else slot
        return remote(src, slot, f_send.at[j, zz], f_recv.at[j, zz], sibling)

    def f_arrived(zz, j):
        q = (me + PLANE - j) % PLANE
        slot = abuf.at[(1 - head) * half_z + zz, q]
        return remote(slot, slot, f_send.at[j, zz], f_recv.at[j, zz], sibling)

    def own_a(zz):
        return pltpu.make_async_copy(cols(zz, me), abuf.at[head * half_z + zz, me], loc_a.at[zz])

    def own_w(c):
        return pltpu.make_async_copy(w_own[c], wbuf.at[z, c], loc_w.at[c])

    @pl.loop(0, half_z)
    def _(zz):
        for j in range(1, PLANE):
            a_copy(zz, j).start()

    @pl.loop(0, half_z)
    def _(zz):
        own_a(zz).start()
        f_copy(zz, 0).start()

    for c in range(2):
        own_w(c).start()
    acc[...] = jnp.zeros_like(acc)

    def w_step(s, forward):
        for c in range(2):
            from_left = z - 1 - s
            from_right = z + 1 + s

            @pl.when(from_left >= 0)
            def _():
                w_copy(from_left, c, right, w_right, False).wait_recv()
                if forward:
                    pl.when(has_right)(lambda: w_copy(from_left, c, right, w_right, False).start())

            @pl.when(from_right <= n_z - 1)
            def _():
                w_copy(from_right, c, left, w_left, False).wait_recv()
                if forward:
                    pl.when(has_left)(lambda: w_copy(from_right, c, left, w_left, False).start())

    @pl.loop(0, n_z - 2)
    def _(s):
        w_step(s, True)

    @pl.loop(0, half_z)
    def _(zz):
        for j in range(1, PLANE):
            a_arrived(zz, j).wait_recv()
            f_copy(zz, j).start()

    for c in range(2):
        own_w(c).wait()

    @pl.loop(0, half_z)
    def _(zz):
        own_a(zz).wait()

    @pl.loop(0, half_z)
    def _(zz):
        for j in range(PLANE):
            f_arrived(zz, j).wait_recv()

    def multiply(block):
        @pl.loop(0, PLANE)
        def _(p):
            for c in range(2):
                acc[p, :, c * width : (c + 1) * width] += jnp.dot(
                    abuf[block, p], wbuf[block, c], preferred_element_type=jnp.float32
                )

    @pl.loop(0, n_z)
    def _(block):
        pl.when((block - z < n_z - 1) & (z - block < n_z - 1))(lambda: multiply(block))

    w_step(n_z - 2, False)
    pl.when(z == 0)(lambda: multiply(n_z - 1))
    pl.when(z == n_z - 1)(lambda: multiply(0))

    def r_copy(j):
        p = (me + j) % PLANE
        return remote(sbuf.at[j - 1], rbuf.at[j - 1], r_send.at[j], r_recv.at[j], chip(p))

    for j in (2, 1, 3):
        sbuf[j - 1] = acc[(me + j) % PLANE].astype(jnp.bfloat16)
        r_copy(j).start()
    total = acc[me]
    for j in (1, 3, 2):
        r_copy(j).wait_recv()
        total += rbuf[j - 1].astype(jnp.float32)
    gbuf[fsdp] = total.astype(jnp.bfloat16)

    def g_copy(zz, dev, send, recv):
        slot = gbuf.at[zz * n_y + y]
        return remote(slot, slot, send.at[zz], recv.at[zz], dev)

    cross = (group, z * n_y + (n_y - 1 - y), head)

    def g_start(zz, to_right, to_left):
        if to_right:
            pl.when(has_right)(lambda: g_copy(zz, right, g_right, g_recv).start())
        if to_left:
            pl.when(has_left)(lambda: g_copy(zz, left, g_left, g_recv).start())
        if n_y == 2:
            g_copy(zz, cross, g_cross, c_recv).start()

    g_start(z, True, True)

    @pl.loop(0, n_z - 1)
    def _(s):
        from_left = z - 1 - s
        from_right = z + 1 + s

        @pl.when(from_left >= 0)
        def _():
            g_copy(from_left, right, g_right, g_recv).wait_recv()
            g_start(from_left, True, False)

        @pl.when(from_right <= n_z - 1)
        def _():
            g_copy(from_right, left, g_left, g_recv).wait_recv()
            g_start(from_right, False, True)

    if n_y == 2:
        @pl.loop(0, n_z)
        def _(zz):
            slot = gbuf.at[zz * n_y + (1 - y)]
            remote(slot, slot, g_cross.at[zz], c_recv.at[zz], cross).wait_recv()

    done = pltpu.make_async_copy(gbuf, out, loc_out)
    done.start()

    for j in range(1, PLANE):
        r_copy(j).wait_send()

    @pl.loop(0, half_z)
    def _(zz):
        for j in range(1, PLANE):
            a_copy(zz, j).wait_send()
        for j in range(PLANE):
            f_copy(zz, j).wait_send()

    @pl.loop(0, n_z)
    def _(block):
        @pl.when((block <= z) & has_right)
        def _():
            for c in range(2):
                w_copy(block, c, right, w_right, False).wait_send()
            g_copy(block, right, g_right, g_recv).wait_send()

        @pl.when((block >= z) & has_left)
        def _():
            for c in range(2):
                w_copy(block, c, left, w_left, False).wait_send()
            g_copy(block, left, g_left, g_recv).wait_send()

        if n_y == 2:
            g_copy(block, cross, g_cross, c_recv).wait_send()

    done.wait()


def project(mesh_sizes, activations, w_key, w_value):
    n_groups, n_fsdp = mesh_sizes
    n_y = PLANE // n_groups
    n_z = n_fsdp // n_y
    rows = activations.shape[0]
    depth, width = w_key.shape
    part = depth // n_groups
    any_space = pl.BlockSpec(memory_space=pl.ANY)
    dma = pltpu.SemaphoreType.DMA
    half_z = n_z // 2
    return pl.pallas_call(
        functools.partial(rows_kernel, n_groups, n_z, n_y),
        out_shape=jax.ShapeDtypeStruct((n_fsdp, rows, 2 * width), jnp.bfloat16),
        in_specs=[any_space] * 3,
        out_specs=any_space,
        scratch_shapes=[
            pltpu.VMEM((n_z, PLANE, rows, part), jnp.bfloat16),
            pltpu.VMEM((n_z, 2, part, width), jnp.bfloat16),
            pltpu.VMEM((PLANE, rows, 2 * width), jnp.float32),
            pltpu.VMEM((PLANE - 1, rows, 2 * width), jnp.bfloat16),
            pltpu.VMEM((PLANE - 1, rows, 2 * width), jnp.bfloat16),
            pltpu.VMEM((n_fsdp, rows, 2 * width), jnp.bfloat16),
            dma((n_z, 2)),
            dma((n_z, 2)),
            dma((n_z, 2)),
            dma((PLANE, half_z)),
            dma((PLANE, half_z)),
            dma((PLANE, half_z)),
            dma((PLANE, half_z)),
            dma((PLANE,)),
            dma((PLANE,)),
            dma((n_z,)),
            dma((n_z,)),
            dma((n_z,)),
            dma((n_z,)),
            dma((n_z,)),
            dma((2,)),
            dma((half_z,)),
            dma,
        ],
        compiler_params=pltpu.CompilerParams(
            collective_id=0, has_side_effects=True, vmem_limit_bytes=48 * 2**20
        ),
    )(activations, w_key, w_value)


def attend_kernel(per_group, info, queries, blocks, attended, cache):
    kv_index, page = pl.program_id(0), pl.program_id(1)
    block_rows = blocks.shape[1]
    width = blocks.shape[2] // 2
    kv_here = width // HD
    my_block = info[0]
    begin = info[1 + page]
    per_block = block_rows // PAGE
    first_block = begin // per_block
    q_pos = (my_block * per_block + page) * PAGE + lax.broadcasted_iota(jnp.int32, (PAGE, 1), 0)
    factor = HD ** -0.5 * 1.4426950408889634

    def run(kv, count):
        k_pos = first_block * block_rows + lax.broadcasted_iota(
            jnp.int32, (1, count * block_rows), 1
        )
        bias = jnp.where((k_pos >= begin * PAGE) & (k_pos <= q_pos), 0.0, -1e30)
        low = kv * HD
        keys = [blocks[first_block + i, :, low : low + HD] for i in range(count)]
        values = [blocks[first_block + i, :, width + low : width + low + HD] for i in range(count)]
        keys = jnp.concatenate(keys, axis=0)
        values = jnp.concatenate(values, axis=0)
        for h in range(per_group):
            at = slice(h * HD, (h + 1) * HD)
            scores = lax.dot_general(
                queries[:, at], keys, (((1,), (1,)), ((), ())), preferred_element_type=jnp.float32
            )
            scores = scores + bias
            top = jnp.max(scores, axis=1, keepdims=True)
            expo = jnp.exp2((scores - top) * factor)
            total = jnp.sum(expo, axis=1, keepdims=True)
            mixed = jnp.dot(expo.astype(jnp.bfloat16), values, preferred_element_type=jnp.float32)
            attended[:, at] = (mixed / total).astype(jnp.bfloat16)

    for kv in range(kv_here):
        for count in range(1, SPAN + 2):
            pl.when((kv_index == kv) & (my_block - first_block == count - 1))(
                functools.partial(run, kv, count)
            )

    @pl.when((kv_index == 0) & (page == 0))
    def _():
        base, pages = info[1 + per_block], info[2 + per_block]
        last = blocks.shape[0] * per_block - 1
        for slot in range(cache.shape[0]):
            source = jnp.minimum(base + slot, last)
            rows = pl.ds(pl.multiple_of((source % per_block) * PAGE, PAGE), PAGE)
            data = blocks[source // per_block, rows, :]
            data = jnp.where(slot < pages, data, jnp.zeros_like(data))
            cache[slot, 0] = data[:, :width]
            cache[slot, 1] = data[:, width:]


def attend(info, queries, gathered, kv_here, cache_pages):
    rows, q_width = queries.shape
    n_blocks, block_rows, width = gathered.shape
    group_width = q_width // kv_here
    return pl.pallas_call(
        functools.partial(attend_kernel, group_width // HD),
        out_shape=(
            jax.ShapeDtypeStruct((rows, q_width), jnp.bfloat16),
            jax.ShapeDtypeStruct((cache_pages, 2, PAGE, width // 2), jnp.bfloat16),
        ),
        grid_spec=pltpu.PrefetchScalarGridSpec(
            num_scalar_prefetch=1,
            grid=(kv_here, rows // PAGE),
            in_specs=[
                pl.BlockSpec((PAGE, group_width), lambda kv, page, info: (page, kv)),
                pl.BlockSpec((n_blocks, block_rows, width), lambda kv, page, info: (0, 0, 0)),
            ],
            out_specs=[
                pl.BlockSpec((PAGE, group_width), lambda kv, page, info: (page, kv)),
                pl.BlockSpec(
                    (cache_pages, 2, PAGE, width // 2), lambda kv, page, info: (0, 0, 0, 0)
                ),
            ],
        ),
        compiler_params=pltpu.CompilerParams(
            dimension_semantics=("arbitrary", "arbitrary"), vmem_limit_bytes=48 * 2**20
        ),
    )(info, queries, gathered)


def per_device(mesh_sizes, activations, queries, w_key, w_value, request_pages, request_owner):
    my_index = lax.axis_index("fsdp")
    gathered = project(mesh_sizes, activations, w_key, w_value)
    pages_here = activations.shape[0] // PAGE
    doc_ends = jnp.cumsum(request_pages)
    doc_begins = doc_ends - request_pages
    own_pages = my_index * pages_here + jnp.arange(pages_here, dtype=jnp.int32)
    inside = (doc_begins[None, :] <= own_pages[:, None]) & (own_pages[:, None] < doc_ends[None, :])
    begins = jnp.sum(jnp.where(inside, doc_begins[None, :], 0), axis=1)
    owned = request_owner == my_index
    base = jnp.sum(jnp.where(owned, doc_begins, 0))
    count = jnp.sum(jnp.where(owned, request_pages, 0))
    info = jnp.concatenate([my_index[None], begins, base[None], count[None]]).astype(jnp.int32)
    return attend(info, queries, gathered, w_key.shape[1] // HD, SPAN * pages_here + 1)


def solution(mesh):
    mesh_sizes = (mesh.shape["groups"], mesh.shape["fsdp"])
    return jax.shard_map(
        functools.partial(per_device, mesh_sizes),
        mesh=mesh,
        in_specs=(
            P(("groups", "fsdp"), "head"),
            P(("groups", "fsdp"), "head"),
            P("fsdp", "head"),
            P("fsdp", "head"),
            P("groups"),
            P("groups"),
        ),
        out_specs=(P(("groups", "fsdp"), "head"), P(("groups", "fsdp"), None, None, "head")),
        check_vma=False,
    )
```

```python
import functools
import jax
import jax.numpy as jnp
from jax import lax
from jax.experimental import pallas as pl
from jax.experimental.pallas import tpu as pltpu
from jax.sharding import PartitionSpec as P

HD = 128
PAGE = 128
SPAN = 3
PLANE = 4


def rows_kernel(
    n_groups, n_z, n_y, acts, w_key, w_value, out, abuf, wbuf, acc, rbuf, gbuf,
    w_right, w_left, w_recv, a_send, a_recv, f_send, f_recv, r_send, r_recv,
    g_right, g_left, g_cross, g_recv, c_recv, loc_w, loc_a, loc_out,
):
    group = lax.axis_index("groups")
    fsdp = lax.axis_index("fsdp")
    head = lax.axis_index("head")
    z = fsdp // n_y
    y = fsdp % n_y
    me = group * n_y + y
    rows = acts.shape[0]
    part = w_key.shape[0] // n_groups
    width = w_key.shape[1]
    half_z = n_z // 2
    sibling = (group, fsdp, 1 - head)
    right = (group, fsdp + n_y, head)
    left = (group, fsdp - n_y, head)
    has_right = z < n_z - 1
    has_left = z > 0

    def chip(p):
        return (p // n_y, z * n_y + p % n_y, head)

    def remote(src, dst, send, recv, dev):
        return pltpu.make_async_remote_copy(
            src_ref=src, dst_ref=dst, send_sem=send, recv_sem=recv,
            device_id=dev, device_id_type=pl.DeviceIdType.MESH,
        )

    barrier = pltpu.get_barrier_semaphore()

    def greet(dev):
        pl.semaphore_signal(barrier, inc=1, device_id=dev, device_id_type=pl.DeviceIdType.MESH)

    for j in range(1, PLANE):
        greet(chip((me + j) % PLANE))
    greet(sibling)
    pl.when(has_right)(lambda: greet(right))
    pl.when(has_left)(lambda: greet(left))
    pl.semaphore_wait(barrier, PLANE + jnp.minimum(z, 1) + jnp.minimum(n_z - 1 - z, 1))

    mine = pl.ds(pl.multiple_of(group * part, part), part)
    w_own = [w_key.at[mine, :], w_value.at[mine, :]]

    def w_copy(block, c, dev, send, own):
        src = w_own[c] if own else wbuf.at[block, c]
        return remote(src, wbuf.at[block, c], send.at[block, c], w_recv.at[block, c], dev)

    def w_own_start(c):
        pl.when(has_right)(lambda: w_copy(z, c, right, w_right, True).start())
        pl.when(has_left)(lambda: w_copy(z, c, left, w_left, True).start())

    w_own_start(0)

    def cols(zz, p):
        start = ((zz * n_y + p % n_y) * n_groups + p // n_y) * part
        return acts.at[:, pl.ds(pl.multiple_of(start, part), part)]

    def a_copy(zz, j):
        p = (me + j) % PLANE
        return remote(
            cols(zz, p), abuf.at[head * half_z + zz, me], a_send.at[j, zz], a_recv.at[j, zz], chip(p)
        )

    def a_arrived(zz, j):
        q = (me + PLANE - j) % PLANE
        return remote(
            cols(zz, me), abuf.at[head * half_z + zz, q], a_send.at[j, zz], a_recv.at[j, zz], chip(q)
        )

    def f_copy(zz, j):
        q = (me + PLANE - j) % PLANE
        slot = abuf.at[head * half_z + zz, q]
        src = cols(zz, me) if j == 0 else slot
        return remote(src, slot, f_send.at[j, zz], f_recv.at[j, zz], sibling)

    def f_arrived(zz, j):
        q = (me + PLANE - j) % PLANE
        slot = abuf.at[(1 - head) * half_z + zz, q]
        return remote(slot, slot, f_send.at[j, zz], f_recv.at[j, zz], sibling)

    def own_a(zz):
        return pltpu.make_async_copy(cols(zz, me), abuf.at[head * half_z + zz, me], loc_a.at[zz])

    def own_w(c):
        return pltpu.make_async_copy(w_own[c], wbuf.at[z, c], loc_w.at[c])

    @pl.loop(0, half_z)
    def _(zz):
        for j in range(1, PLANE):
            a_copy(zz, j).start()

    @pl.loop(0, half_z)
    def _(zz):
        own_a(zz).start()
        f_copy(zz, 0).start()

    for c in range(2):
        own_w(c).start()
    acc[...] = jnp.zeros_like(acc)

    at_end = jnp.logical_not(has_right & has_left)

    def relay(s, c):
        from_left = z - 1 - s
        from_right = z + 1 + s

        @pl.when((from_left >= 0) & has_right)
        def _():
            w_copy(from_left, c, right, w_right, False).wait_recv()
            w_copy(from_left, c, right, w_right, False).start()

        @pl.when((from_right <= n_z - 1) & has_left)
        def _():
            w_copy(from_right, c, left, w_left, False).wait_recv()
            w_copy(from_right, c, left, w_left, False).start()

    relay(0, 0)
    w_own_start(1)

    @pl.loop(1, n_z - 2)
    def _(s):
        relay(s, 0)

    @pl.loop(0, n_z - 2)
    def _(s):
        relay(s, 1)

    @pl.loop(0, half_z)
    def _(zz):
        for j in range(1, PLANE):
            a_arrived(zz, j).wait_recv()
            f_copy(zz, j).start()

    for c in range(2):
        own_w(c).wait()

    @pl.loop(0, half_z)
    def _(zz):
        own_a(zz).wait()

    @pl.loop(0, half_z)
    def _(zz):
        for j in range(PLANE):
            f_arrived(zz, j).wait_recv()

    def multiply(i, c):
        block = jnp.where(z == 0, i, n_z - 1 - i)

        @pl.when(at_end & (block != z))
        def _():
            w_copy(block, c, right, w_right, False).wait_recv()

        @pl.loop(0, PLANE)
        def _(p):
            acc[c, p] += jnp.dot(
                abuf[block, p], wbuf[block, c], preferred_element_type=jnp.float32
            )

    def r_copy(j, c):
        p = (me + j) % PLANE
        return remote(acc.at[c, p], rbuf.at[c, j - 1], r_send.at[c, j], r_recv.at[c, j], chip(p))

    def r_start(c):
        for j in (2, 1, 3):
            r_copy(j, c).start()

    def g_copy(zz, c, dev, send, recv):
        slot = gbuf.at[zz * n_y + y, :, pl.ds(c * width, width)]
        return remote(slot, slot, send.at[zz, c], recv.at[zz, c], dev)

    cross = (group, z * n_y + (n_y - 1 - y), head)

    def g_start(zz, c, to_right, to_left):
        if to_right:
            pl.when(has_right)(lambda: g_copy(zz, c, right, g_right, g_recv).start())
        if to_left:
            pl.when(has_left)(lambda: g_copy(zz, c, left, g_left, g_recv).start())
        if n_y == 2:
            g_copy(zz, c, cross, g_cross, c_recv).start()

    def r_finish(c):
        total = acc[c, me]
        for j in (1, 3, 2):
            r_copy(j, c).wait_recv()
            total += rbuf[c, j - 1]
        gbuf[fsdp, :, c * width : (c + 1) * width] = total.astype(jnp.bfloat16)
        g_start(z, c, True, True)

    def g_relay(c):
        @pl.loop(0, n_z - 1)
        def _(s):
            from_left = z - 1 - s
            from_right = z + 1 + s

            @pl.when(from_left >= 0)
            def _():
                g_copy(from_left, c, right, g_right, g_recv).wait_recv()
                g_start(from_left, c, True, False)

            @pl.when(from_right <= n_z - 1)
            def _():
                g_copy(from_right, c, left, g_left, g_recv).wait_recv()
                g_start(from_right, c, False, True)

    @pl.loop(0, n_z)
    def _(i):
        multiply(i, 0)

    r_start(0)

    @pl.loop(0, n_z - 1)
    def _(i):
        multiply(i, 1)

    r_finish(0)
    multiply(n_z - 1, 1)
    r_start(1)
    g_relay(0)
    r_finish(1)
    g_relay(1)

    if n_y == 2:
        @pl.loop(0, n_z)
        def _(zz):
            for c in range(2):
                slot = gbuf.at[zz * n_y + (1 - y), :, pl.ds(c * width, width)]
                remote(slot, slot, g_cross.at[zz, c], c_recv.at[zz, c], cross).wait_recv()

    done = pltpu.make_async_copy(gbuf, out, loc_out)
    done.start()

    for c in range(2):
        for j in range(1, PLANE):
            r_copy(j, c).wait_send()

    @pl.loop(0, half_z)
    def _(zz):
        for j in range(1, PLANE):
            a_copy(zz, j).wait_send()
        for j in range(PLANE):
            f_copy(zz, j).wait_send()

    @pl.loop(0, n_z)
    def _(block):
        for c in range(2):
            @pl.when((block <= z) & has_right)
            def _():
                w_copy(block, c, right, w_right, False).wait_send()
                g_copy(block, c, right, g_right, g_recv).wait_send()

            @pl.when((block >= z) & has_left)
            def _():
                w_copy(block, c, left, w_left, False).wait_send()
                g_copy(block, c, left, g_left, g_recv).wait_send()

            if n_y == 2:
                g_copy(block, c, cross, g_cross, c_recv).wait_send()

    done.wait()


def project(mesh_sizes, activations, w_key, w_value):
    n_groups, n_fsdp = mesh_sizes
    n_y = PLANE // n_groups
    n_z = n_fsdp // n_y
    rows = activations.shape[0]
    depth, width = w_key.shape
    part = depth // n_groups
    any_space = pl.BlockSpec(memory_space=pl.ANY)
    dma = pltpu.SemaphoreType.DMA
    half_z = n_z // 2
    return pl.pallas_call(
        functools.partial(rows_kernel, n_groups, n_z, n_y),
        out_shape=jax.ShapeDtypeStruct((n_fsdp, rows, 2 * width), jnp.bfloat16),
        in_specs=[any_space] * 3,
        out_specs=any_space,
        scratch_shapes=[
            pltpu.VMEM((n_z, PLANE, rows, part), jnp.bfloat16),
            pltpu.VMEM((n_z, 2, part, width), jnp.bfloat16),
            pltpu.VMEM((2, PLANE, rows, width), jnp.float32),
            pltpu.VMEM((2, PLANE - 1, rows, width), jnp.float32),
            pltpu.VMEM((n_fsdp, rows, 2 * width), jnp.bfloat16),
            dma((n_z, 2)),
            dma((n_z, 2)),
            dma((n_z, 2)),
            dma((PLANE, half_z)),
            dma((PLANE, half_z)),
            dma((PLANE, half_z)),
            dma((PLANE, half_z)),
            dma((2, PLANE)),
            dma((2, PLANE)),
            dma((n_z, 2)),
            dma((n_z, 2)),
            dma((n_z, 2)),
            dma((n_z, 2)),
            dma((n_z, 2)),
            dma((2,)),
            dma((half_z,)),
            dma,
        ],
        compiler_params=pltpu.CompilerParams(
            collective_id=0, has_side_effects=True, vmem_limit_bytes=60 * 2**20
        ),
    )(activations, w_key, w_value)


def attend_kernel(per_group, request_pages, request_owner, queries, blocks, attended, cache):
    kv_index, page = pl.program_id(0), pl.program_id(1)
    block_rows = blocks.shape[1]
    width = blocks.shape[2] // 2
    kv_here = width // HD
    my_block = lax.axis_index("fsdp")
    per_block = block_rows // PAGE
    own_page = my_block * per_block + page

    def request(r, carry):
        end, begin, base, pages = carry
        count = request_pages[r]
        owned = request_owner[r] == my_block
        begin = jnp.where(end <= own_page, end, begin)
        base = jnp.where(owned, end, base)
        pages = jnp.where(owned, count, pages)
        return end + count, begin, base, pages

    zero = jnp.int32(0)
    _, begin, base, pages = lax.fori_loop(
        0, request_pages.shape[0], request, (zero, zero, zero, zero)
    )
    first_block = begin // per_block
    q_pos = own_page * PAGE + lax.broadcasted_iota(jnp.int32, (PAGE, 1), 0)
    factor = HD ** -0.5 * 1.4426950408889634

    def run(kv, count):
        k_pos = first_block * block_rows + lax.broadcasted_iota(
            jnp.int32, (1, count * block_rows), 1
        )
        bias = jnp.where((k_pos >= begin * PAGE) & (k_pos <= q_pos), 0.0, -1e30)
        low = kv * HD
        keys = [blocks[first_block + i, :, low : low + HD] for i in range(count)]
        values = [blocks[first_block + i, :, width + low : width + low + HD] for i in range(count)]
        keys = jnp.concatenate(keys, axis=0)
        values = jnp.concatenate(values, axis=0)
        for h in range(per_group):
            at = slice(h * HD, (h + 1) * HD)
            scores = lax.dot_general(
                queries[:, at], keys, (((1,), (1,)), ((), ())), preferred_element_type=jnp.float32
            )
            scores = scores + bias
            top = jnp.max(scores, axis=1, keepdims=True)
            expo = jnp.exp2((scores - top) * factor)
            total = jnp.sum(expo, axis=1, keepdims=True)
            mixed = jnp.dot(expo.astype(jnp.bfloat16), values, preferred_element_type=jnp.float32)
            attended[:, at] = (mixed / total).astype(jnp.bfloat16)

    for kv in range(kv_here):
        for count in range(1, SPAN + 2):
            pl.when((kv_index == kv) & (my_block - first_block == count - 1))(
                functools.partial(run, kv, count)
            )

    @pl.when((kv_index == 0) & (page == 0))
    def _():
        last = blocks.shape[0] * per_block - 1
        for slot in range(cache.shape[0]):
            source = jnp.minimum(base + slot, last)
            rows = pl.ds(pl.multiple_of((source % per_block) * PAGE, PAGE), PAGE)
            data = blocks[source // per_block, rows, :]
            data = jnp.where(slot < pages, data, jnp.zeros_like(data))
            cache[slot, 0] = data[:, :width]
            cache[slot, 1] = data[:, width:]


def attend(request_pages, request_owner, queries, gathered, kv_here, cache_pages):
    rows, q_width = queries.shape
    n_blocks, block_rows, width = gathered.shape
    group_width = q_width // kv_here
    return pl.pallas_call(
        functools.partial(attend_kernel, group_width // HD),
        out_shape=(
            jax.ShapeDtypeStruct((rows, q_width), jnp.bfloat16),
            jax.ShapeDtypeStruct((cache_pages, 2, PAGE, width // 2), jnp.bfloat16),
        ),
        grid_spec=pltpu.PrefetchScalarGridSpec(
            num_scalar_prefetch=2,
            grid=(kv_here, rows // PAGE),
            in_specs=[
                pl.BlockSpec((PAGE, group_width), lambda kv, page, *_: (page, kv)),
                pl.BlockSpec((n_blocks, block_rows, width), lambda kv, page, *_: (0, 0, 0)),
            ],
            out_specs=[
                pl.BlockSpec((PAGE, group_width), lambda kv, page, *_: (page, kv)),
                pl.BlockSpec(
                    (cache_pages, 2, PAGE, width // 2), lambda kv, page, *_: (0, 0, 0, 0)
                ),
            ],
        ),
        compiler_params=pltpu.CompilerParams(
            dimension_semantics=("arbitrary", "arbitrary"), vmem_limit_bytes=48 * 2**20
        ),
    )(request_pages, request_owner, queries, gathered)


def per_device(mesh_sizes, activations, queries, w_key, w_value, request_pages, request_owner):
    gathered = project(mesh_sizes, activations, w_key, w_value)
    cache_pages = SPAN * (activations.shape[0] // PAGE) + 1
    kv_here = w_key.shape[1] // HD
    return attend(request_pages, request_owner, queries, gathered, kv_here, cache_pages)


def solution(mesh):
    mesh_sizes = (mesh.shape["groups"], mesh.shape["fsdp"])
    return jax.shard_map(
        functools.partial(per_device, mesh_sizes),
        mesh=mesh,
        in_specs=(
            P(("groups", "fsdp"), "head"),
            P(("groups", "fsdp"), "head"),
            P("fsdp", "head"),
            P("fsdp", "head"),
            P("groups"),
            P("groups"),
        ),
        out_specs=(P(("groups", "fsdp"), "head"), P(("groups", "fsdp"), None, None, "head")),
        check_vma=False,
    )
```
